32 devices in a mesh: item: 4 (over y, core), user: 8 (over z, x).
Axes of the slice: x: 2, y: 2, z: 4, core: 2. Of those that a mesh axis runs over, the one named last changes fastest.
Arguments:
- item_factors: float32 [8192, 128], P('item')
- tile_lists: int32 [32, 16], P(('item', 'user')), may hold values from 0 to 63, as said below
- tile_weights: bfloat16 [32, 16, 128, 128], P(('item', 'user')), may hold values from 0 to 40
- user_factors: float32 [4096, 128], P(('item', 'user')), may hold values from -6 to 6
Outputs:
- new_factors: float32 [4096, 128], P(('item', 'user'))
The draws below stay inside these ranges and needn't reach their ends.
Inputs may be any that keep to these rules, and one draw needn't show every extreme that they name: `tile_lists`: item shard s holds tiles s * 16 to (s + 1) * 16 - 1. Among the 16 slots of one device's blocks, at most 8 name tiles of one item shard, and for some shard exactly 8 do; a tile may be named more than once.
All inputs are finite; a program needn't handle non-finite values.
Results may differ from the reference program's by a relative error of at most 0.0024.
Values sent between devices are 32-bit elements; how exact they have to be, the bound alone decides.
A program may use at most 64 MiB of HBM per device.

```python
import math
import jax
import jax.numpy as jnp
from jax import lax

R = 128
TILE = 128
BLK_DEV = 1
K = 16
ITILES_DEV = 16
ITERS = 4
BLOCKS = 32
USERS = 4096
ITEM_TILES = 64
ITEMS = 8192


def draw_item_factors(key, part):
    first, second, third = jax.random.split(key, 3)
    base = jax.random.normal(first, (ITEMS, R), jnp.float32)
    columns = jnp.exp(jax.random.uniform(second, (1, R), jnp.float32, math.log(0.3), math.log(3.0)))
    rising = jnp.sqrt(1.0 + 2.0 * jnp.arange(ITEMS, dtype=jnp.float32)[:, None] / ITEMS)
    row_scale = jnp.exp(jax.random.uniform(third, (ITEMS, 1), jnp.float32, math.log(0.3), math.log(3.0))) * rising
    return (base * row_scale * columns * (1.0 / math.sqrt(ITEMS))).astype(jnp.float32)


def draw_tile_lists(key, part):
    devices_total = BLOCKS // BLK_DEV
    slots_total = BLK_DEV * K
    shards_total = ITEM_TILES // ITILES_DEV
    capacity = 2 * slots_total // shards_total

    def device_list(dev_key):
        hot_key, pool_key, order_key, pick_key = jax.random.split(dev_key, 4)
        hot_shard = jax.random.randint(hot_key, (), 0, shards_total)
        pool = jax.random.permutation(pool_key, (shards_total - 1) * capacity)[:slots_total - capacity]
        others = pool // capacity
        others = jnp.where(others >= hot_shard, others + 1, others)
        owners = jnp.concatenate([jnp.full((capacity,), hot_shard, jnp.int32), others.astype(jnp.int32)])
        owners = owners[jax.random.permutation(order_key, slots_total)]
        offsets = jax.random.randint(pick_key, (slots_total,), 0, ITILES_DEV)
        return (owners * ITILES_DEV + offsets).astype(jnp.int32)
    keys = jax.random.split(jax.random.fold_in(key, 7), devices_total)
    return jax.vmap(device_list)(keys).reshape(BLOCKS, K)


def shard_levels(key, shape, pieces, least, high):
    gain = 1.0
    for axis_at, parts in pieces:
        steps = jax.random.uniform(jax.random.fold_in(jax.random.fold_in(key, 6), axis_at), (parts,), jnp.float32, least / len(pieces), high / len(pieces))
        gain = gain * jnp.repeat(jnp.exp(steps), shape[axis_at] // parts).reshape((-1,) + (1,) * (len(shape) - 1 - axis_at))
    return gain


def scatter_about(key, extent, deviation, bound, pieces=(), kind=jnp.bfloat16):
    loudness = shard_levels(key, extent, pieces, -0.22, 0.18) if pieces else 1.0
    drawn = jax.random.normal(key, extent, jnp.float32) * deviation * loudness
    return jnp.minimum(jnp.maximum(drawn, -bound), bound).astype(kind)


def setup_inputs(seed: int = 0) -> dict:
    streams_of = jax.random.split(jax.random.key(seed), 5)
    return {
        "item_factors": draw_item_factors(jax.random.fold_in(streams_of[4], 71), 0),
        "tile_lists": draw_tile_lists(jax.random.fold_in(streams_of[4], 71), 0),
        "tile_weights": jnp.clip(40.0 * jax.random.uniform(streams_of[2], (BLOCKS, K, TILE, TILE), jnp.float32) ** shard_levels(streams_of[2], (BLOCKS, K, TILE, TILE), ((0, 32),), -0.2, 0.2), 0.0, 40.0).astype(jnp.bfloat16),
        "user_factors": scatter_about(streams_of[3], (USERS, R), 1.0, 6.0, ((0, 32),), jnp.float32),
    }


RIDGE_WEIGHT = 0.1
EPSILON = 1e-6
HIGHEST = lax.Precision.HIGHEST


def apply_system(vectors, tiles, weights, gram):
    scores = jnp.einsum('bur,bkir->bkui', vectors, tiles, precision=HIGHEST)
    spread = jnp.einsum('bkui,bkir->bur', scores * weights, tiles, precision=HIGHEST)
    return spread + jnp.einsum('bur,rs->bus', vectors, gram, precision=HIGHEST) + RIDGE_WEIGHT * vectors


def conjugate(start, tiles, weights, gram, steps):
    weights = weights.astype(jnp.float32)
    target = jnp.einsum('bkui,bkir->bur', 1.0 + weights, tiles, precision=HIGHEST)
    answer = start
    resid = target - apply_system(start, tiles, weights, gram)
    direction = resid
    norm_now = jnp.sum(resid * resid, axis=-1, keepdims=True)
    for step_index in range(steps):
        image = apply_system(direction, tiles, weights, gram)
        alpha = norm_now / (jnp.sum(direction * image, axis=-1, keepdims=True) + EPSILON)
        answer = answer + alpha * direction
        resid = resid - alpha * image
        norm_next = jnp.sum(resid * resid, axis=-1, keepdims=True)
        direction = resid + (norm_next / (norm_now + EPSILON)) * direction
        norm_now = norm_next
    return answer


def reference(item_factors, tile_lists, tile_weights, user_factors):
    gram = jnp.dot(item_factors.T, item_factors, precision=HIGHEST, preferred_element_type=jnp.float32)
    all_tiles = item_factors.reshape(ITEM_TILES, TILE, R)

    def block_solve(packed):
        tile_ids, weights, start = packed
        tiles = all_tiles[tile_ids][None]
        return conjugate(start[None], tiles, weights[None], gram, ITERS)[0]

    solved = lax.map(block_solve, (tile_lists, tile_weights, user_factors.reshape(BLOCKS, TILE, R)))
    return solved.reshape(USERS, R)
```

```python
import functools

import jax
import jax.numpy as jnp
from jax import lax
from jax.experimental import pallas as pl
from jax.experimental.pallas import tpu as pltpu
from jax.sharding import PartitionSpec as P

ITERS = 4
RIDGE_WEIGHT = 0.1
EPSILON = 1e-06
ROWS = 16
GROUP = 2
MESH = pl.DeviceIdType.MESH
F32 = jnp.float32
BF16 = jnp.bfloat16


def split(value):
    high = value.astype(BF16)
    low = (value - high.astype(F32)).astype(BF16)
    return high, low


def beside(value):
    return jnp.concatenate(split(value), axis=1)


def stacked(value):
    pair = beside(value)
    return jnp.concatenate([pair, pair], axis=0)


def dot(a, b):
    return jnp.dot(a, b, preferred_element_type=F32)


def fold_columns(value):
    half = value.shape[1] // 2
    return value[:, :half] + value[:, half:]


def fold_rows(value):
    half = value.shape[0] // 2
    return value[:half] + value[half:]


def kernel(items, stages, lists_ref, shard_ref, w_ref, u_ref, out_ref, *scratch):
    bufs = scratch[:stages]
    (w_vm, u_vm, w_t, y_hl, y_t, in_sem, own_sem, sib_send, sib_recv, y_send, y_recv,
     x_send, x_recv, f_send, f_recv) = scratch[stages:]
    tiles = shard_ref.shape[0]
    slots = w_ref.shape[0]
    rank = shard_ref.shape[2]
    ny = items // 2
    piece = ROWS // GROUP

    me = lax.axis_index("item")
    user = lax.axis_index("user")
    y, core = me // 2, lax.rem(me, 2)
    sibling = y * 2 + (1 - core)
    g = lax.rem(user, GROUP)
    peer = user - g + (1 - g)
    sib_id = (sibling, user)
    peer_id = (me, peer)

    w_copy = pltpu.make_async_copy(w_ref, w_vm, in_sem.at[0])
    u_copy = pltpu.make_async_copy(u_ref, u_vm, in_sem.at[1])
    w_copy.start()
    u_copy.start()

    def y_id(step):
        return (lax.rem(y + step, ny) * 2 + core, user)

    barrier = pltpu.get_barrier_semaphore()
    pl.semaphore_signal(barrier, inc=1, device_id=sib_id, device_id_type=MESH)
    pl.semaphore_signal(barrier, inc=1, device_id=peer_id, device_id_type=MESH)
    for step in range(1, ny):
        pl.semaphore_signal(barrier, inc=1, device_id=y_id(step), device_id_type=MESH)
    pl.semaphore_wait(barrier, 1 + ny)

    def remote(src, dst, send, recv, device):
        return pltpu.make_async_remote_copy(
            src_ref=src, dst_ref=dst, send_sem=send, recv_sem=recv,
            device_id=device, device_id_type=MESH)

    def region(m, shard, part=None):
        span = pl.ds(pl.multiple_of(shard * tiles, tiles), tiles)
        if part is None:
            return bufs[m].at[span]
        return bufs[m].at[span, pl.ds(pl.multiple_of(part * piece, piece), piece)]

    def far(step):
        return lax.rem(y + ny - step, ny) * 2 + core

    def far_sib(step):
        return lax.rem(y + ny - step, ny) * 2 + (1 - core)

    def y_copy(m, step):
        rows = pl.ds(pl.multiple_of(m * ROWS + g * piece, piece), piece)
        return remote(shard_ref.at[:, rows], region(m, me, g),
                      y_send.at[step - 1, m], y_recv.at[step - 1, m], y_id(step))

    def y_arrival(m, step):
        place = region(m, far(step), g)
        return remote(place, place, y_send.at[step - 1, m], y_recv.at[step - 1, m], y_id(step))

    def x_copy(m, step, part):
        place = region(m, far(step), part)
        return remote(place, place, x_send.at[step - 1, m], x_recv.at[step - 1, m], peer_id)

    def f_copy(m, step, which, shard, part):
        place = region(m, shard, part)
        return remote(place, place, f_send.at[step - 1, which, m], f_recv.at[step - 1, which, m], sib_id)

    def own_to_sib(m):
        return remote(shard_ref.at[:, pl.ds(m * ROWS, ROWS)], region(m, me),
                      sib_send.at[m], sib_recv.at[m], sib_id)

    def own_copy(m):
        return pltpu.make_async_copy(shard_ref.at[:, pl.ds(m * ROWS, ROWS)], region(m, me), own_sem.at[m])

    for m in range(stages):
        for step in range(1, ny):
            y_copy(m, step).start()
        own_to_sib(m).start()
        own_copy(m).start()

    w_copy.wait()
    for k in range(slots):
        turned = w_vm[k].astype(F32).T
        for m in range(stages):
            w_t[m, k * ROWS:(k + 1) * ROWS, :] = turned[m * ROWS:(m + 1) * ROWS]
    u_copy.wait()
    answer = u_vm[...].T
    start_pair = stacked(answer)

    def spread_of(m, rows_hl, columns_t, vectors):
        scores = fold_columns(dot(rows_hl, vectors))
        return dot(columns_t, beside(scores * w_t[m]))

    gram = jnp.zeros((2 * rank, 2 * rank), F32)
    first = jnp.zeros((2 * rank, 2 * rank), F32)
    target = jnp.zeros((2 * rank, 2 * rank), F32)
    for turn in range(stages + 2):
        if turn < stages:
            for step in range(1, ny):
                y_arrival(turn, step).wait_recv()
                x_copy(turn, step, g).start()
                f_copy(turn, step, 0, far(step), g).start()
        if 1 <= turn <= stages:
            for step in range(1, ny):
                x_copy(turn - 1, step, 1 - g).wait_recv()
                f_copy(turn - 1, step, 1, far(step), 1 - g).start()
        if turn >= 2:
            m = turn - 2
            own_copy(m).wait()
            place = region(m, sibling)
            remote(place, place, sib_send.at[m], sib_recv.at[m], sib_id).wait_recv()
            for step in range(1, ny):
                f_copy(m, step, 0, far_sib(step), g).wait_recv()
                f_copy(m, step, 1, far_sib(step), 1 - g).wait_recv()
            every = beside(bufs[m][...].reshape(-1, rank))
            gram += lax.dot_general(every, every, (((0,), (0,)), ((), ())), preferred_element_type=F32)
            rows = jnp.concatenate([bufs[m][lists_ref[0, k]] for k in range(slots)], axis=0)
            rows_hl = beside(rows)
            columns_t = jnp.concatenate(split(rows.T), axis=0)
            y_hl[m] = rows_hl
            y_t[m] = columns_t
            first += spread_of(m, rows_hl, columns_t, start_pair)
            weights = w_t[m].astype(BF16)
            target += dot(columns_t, jnp.concatenate([weights, jnp.ones_like(weights)], axis=1))

    gram_hl = beside(fold_rows(fold_columns(gram)))

    def finish(spread, vectors, pair):
        return fold_rows(fold_columns(spread)) + fold_columns(dot(gram_hl, pair)) + RIDGE_WEIGHT * vectors

    resid = fold_rows(fold_columns(target)) - finish(first, answer, start_pair)
    direction = resid
    norm_now = jnp.sum(resid * resid, axis=0, keepdims=True)
    for index in range(ITERS):
        pair = stacked(direction)
        spread = jnp.zeros((2 * rank, 2 * rank), F32)
        for m in range(stages):
            spread += spread_of(m, y_hl[m], y_t[m], pair)
        image = finish(spread, direction, pair)
        alpha = norm_now / (jnp.sum(direction * image, axis=0, keepdims=True) + EPSILON)
        answer = answer + alpha * direction
        if index + 1 < ITERS:
            resid = resid - alpha * image
            norm_next = jnp.sum(resid * resid, axis=0, keepdims=True)
            direction = resid + norm_next / (norm_now + EPSILON) * direction
            norm_now = norm_next
    out_ref[...] = answer.T

    for m in range(stages):
        own_to_sib(m).wait_send()
        for step in range(1, ny):
            y_copy(m, step).wait_send()
            x_copy(m, step, g).wait_send()
            f_copy(m, step, 0, far(step), g).wait_send()
            f_copy(m, step, 1, far(step), 1 - g).wait_send()


def local(items, item_factors, tile_lists, tile_weights, user_factors):
    rank = item_factors.shape[1]
    side = tile_weights.shape[-1]
    slots = tile_lists.shape[1]
    stages = side // ROWS
    far = items // 2 - 1
    shard = item_factors.reshape(-1, side, rank)
    tiles = shard.shape[0]
    dma = pltpu.SemaphoreType.DMA
    scratch = [pltpu.VMEM((items * tiles, ROWS, rank), F32) for _ in range(stages)]
    scratch += [
        pltpu.VMEM((slots, side, side), BF16),
        pltpu.VMEM((side, rank), F32),
        pltpu.VMEM((stages, slots * ROWS, side), F32),
        pltpu.VMEM((stages, slots * ROWS, 2 * rank), BF16),
        pltpu.VMEM((stages, 2 * rank, slots * ROWS), BF16),
        dma((2,)), dma((stages,)), dma((stages,)), dma((stages,)),
        dma((far, stages)), dma((far, stages)), dma((far, stages)), dma((far, stages)),
        dma((far, 2, stages)), dma((far, 2, stages)),
    ]
    hbm = pl.BlockSpec(memory_space=pl.ANY)
    return pl.pallas_call(
        functools.partial(kernel, items, stages),
        out_shape=jax.ShapeDtypeStruct((side, rank), F32),
        in_specs=[pl.BlockSpec(memory_space=pltpu.SMEM), hbm, hbm, hbm],
        out_specs=pl.BlockSpec(memory_space=pltpu.VMEM),
        scratch_shapes=scratch,
        compiler_params=pltpu.CompilerParams(
            collective_id=0, has_side_effects=True, vmem_limit_bytes=48 * 1024 * 1024),
        name="half_sweep",
    )(tile_lists, shard, tile_weights.reshape(slots, side, side), user_factors)


def solution(mesh):
    in_specs = (
        P("item", None),
        P(("item", "user"), None),
        P(("item", "user"), None, None, None),
        P(("item", "user"), None),
    )
    out_specs = P(("item", "user"), None)
    body = functools.partial(local, mesh.shape["item"])
    return jax.shard_map(body, mesh=mesh, in_specs=in_specs, out_specs=out_specs, check_vma=False)
```

```python
import functools

import jax
import jax.numpy as jnp
from jax import lax
from jax.experimental import pallas as pl
from jax.experimental.pallas import tpu as pltpu
from jax.sharding import PartitionSpec as P

ITERS = 4
RIDGE_WEIGHT = 0.1
EPSILON = 1e-06
ROWS = 16
GROUP = 2
MESH = pl.DeviceIdType.MESH
F32 = jnp.float32
BF16 = jnp.bfloat16


def split(value):
    high = value.astype(BF16)
    low = (value - high.astype(F32)).astype(BF16)
    return high, low


def beside(value):
    return jnp.concatenate(split(value), axis=1)


def stacked(value):
    pair = beside(value)
    return jnp.concatenate([pair, pair], axis=0)


def dot(a, b):
    return jnp.dot(a, b, preferred_element_type=F32)


def fold_columns(value):
    half = value.shape[1] // 2
    return value[:, :half] + value[:, half:]


def fold_rows(value):
    half = value.shape[0] // 2
    return value[:half] + value[half:]


def kernel(items, stages, lists_hbm, shard_ref, w_ref, u_ref, out_ref, *scratch):
    bufs = scratch[:stages]
    (lists_ref, w_vm, u_vm, w_t, y_hl, y_t, in_sem, own_sem, sib_send, sib_recv, y_send, y_recv,
     x_send, x_recv, f_send, f_recv) = scratch[stages:]
    tiles = shard_ref.shape[0]
    slots = w_ref.shape[0]
    rank = shard_ref.shape[2]
    ny = items // 2
    piece = ROWS // GROUP
    part_rows = slots * ROWS
    all_rows = stages * part_rows

    me = lax.axis_index("item")
    user = lax.axis_index("user")
    y, core = me // 2, lax.rem(me, 2)
    sibling = y * 2 + (1 - core)
    g = lax.rem(user, GROUP)
    peer = user - g + (1 - g)
    sib_id = (sibling, user)
    peer_id = (me, peer)

    w_copy = pltpu.make_async_copy(w_ref, w_vm, in_sem.at[0])
    u_copy = pltpu.make_async_copy(u_ref, u_vm, in_sem.at[1])
    lists_copy = pltpu.make_async_copy(lists_hbm, lists_ref, in_sem.at[2])
    w_copy.start()
    u_copy.start()
    lists_copy.start()

    def y_id(step):
        return (lax.rem(y + step, ny) * 2 + core, user)

    barrier = pltpu.get_barrier_semaphore()
    pl.semaphore_signal(barrier, inc=1, device_id=sib_id, device_id_type=MESH)
    pl.semaphore_signal(barrier, inc=1, device_id=peer_id, device_id_type=MESH)
    for step in range(1, ny):
        pl.semaphore_signal(barrier, inc=1, device_id=y_id(step), device_id_type=MESH)
    pl.semaphore_wait(barrier, 1 + ny)

    def remote(src, dst, send, recv, device):
        return pltpu.make_async_remote_copy(
            src_ref=src, dst_ref=dst, send_sem=send, recv_sem=recv,
            device_id=device, device_id_type=MESH)

    def region(m, shard, part=None):
        span = pl.ds(pl.multiple_of(shard * tiles, tiles), tiles)
        if part is None:
            return bufs[m].at[span]
        return bufs[m].at[span, pl.ds(pl.multiple_of(part * piece, piece), piece)]

    def far(step):
        return lax.rem(y + ny - step, ny) * 2 + core

    def far_sib(step):
        return lax.rem(y + ny - step, ny) * 2 + (1 - core)

    def y_copy(m, step):
        rows = pl.ds(pl.multiple_of(m * ROWS + g * piece, piece), piece)
        return remote(shard_ref.at[:, rows], region(m, me, g),
                      y_send.at[step - 1, m], y_recv.at[step - 1, m], y_id(step))

    def y_arrival(m, step):
        place = region(m, far(step), g)
        return remote(place, place, y_send.at[step - 1, m], y_recv.at[step - 1, m], y_id(step))

    def x_copy(m, step, part):
        place = region(m, far(step), part)
        return remote(place, place, x_send.at[step - 1, m], x_recv.at[step - 1, m], peer_id)

    def f_copy(m, step, which, shard, part):
        place = region(m, shard, part)
        return remote(place, place, f_send.at[step - 1, which, m], f_recv.at[step - 1, which, m], sib_id)

    def own_to_sib(m):
        return remote(shard_ref.at[:, pl.ds(m * ROWS, ROWS)], region(m, me),
                      sib_send.at[m], sib_recv.at[m], sib_id)

    def own_copy(m):
        return pltpu.make_async_copy(shard_ref.at[:, pl.ds(m * ROWS, ROWS)], region(m, me), own_sem.at[m])

    for m in range(stages):
        for step in range(1, ny):
            y_copy(m, step).start()
        own_to_sib(m).start()
        own_copy(m).start()

    w_copy.wait()
    for k in range(slots):
        turned = w_vm[k].astype(F32).T
        for m in range(stages):
            w_t[m * part_rows + k * ROWS:m * part_rows + (k + 1) * ROWS] = turned[m * ROWS:(m + 1) * ROWS]
    u_copy.wait()
    lists_copy.wait()
    answer = u_vm[...].T
    start_pair = stacked(answer)

    gram = jnp.zeros((rank, 2 * rank), F32)
    first = jnp.zeros((2 * rank, 2 * rank), F32)
    for turn in range(stages + 2):
        if turn < stages:
            for step in range(1, ny):
                y_arrival(turn, step).wait_recv()
                x_copy(turn, step, g).start()
                f_copy(turn, step, 0, far(step), g).start()
        if 1 <= turn <= stages:
            for step in range(1, ny):
                x_copy(turn - 1, step, 1 - g).wait_recv()
                f_copy(turn - 1, step, 1, far(step), 1 - g).start()
        if turn >= 2:
            m = turn - 2
            own_copy(m).wait()
            place = region(m, sibling)
            remote(place, place, sib_send.at[m], sib_recv.at[m], sib_id).wait_recv()
            for step in range(1, ny):
                f_copy(m, step, 0, far_sib(step), g).wait_recv()
                f_copy(m, step, 1, far_sib(step), 1 - g).wait_recv()
            every, rest = split(bufs[m][...].reshape(-1, rank))
            gram += lax.dot_general(
                every, jnp.concatenate([every, rest], axis=1), (((0,), (0,)), ((), ())), preferred_element_type=F32)
            rows = jnp.concatenate([bufs[m][lists_ref[0, k]] for k in range(slots)], axis=0)
            rows_hl = beside(rows)
            columns_t = jnp.concatenate(split(rows.T), axis=0)
            span = slice(m * part_rows, (m + 1) * part_rows)
            y_hl[span] = rows_hl
            y_t[:, span] = columns_t
            scores = fold_columns(dot(rows_hl, start_pair))
            first += dot(columns_t, beside(1.0 + w_t[span] * (1.0 - scores)))

    gram_hl = beside(gram[:, :rank] + gram[:, rank:] + gram[:, rank:].T)
    y_hl[all_rows:] = gram_hl
    resid = fold_rows(fold_columns(first)) - fold_columns(dot(gram_hl, start_pair)) - RIDGE_WEIGHT * answer
    direction = resid
    norm_now = jnp.sum(resid * resid, axis=0, keepdims=True)
    for index in range(ITERS):
        scores = fold_columns(dot(y_hl[...], stacked(direction)))
        spread = dot(y_t[...], beside(scores[:all_rows] * w_t[...]))
        image = fold_rows(fold_columns(spread)) + scores[all_rows:] + RIDGE_WEIGHT * direction
        alpha = norm_now / (jnp.sum(direction * image, axis=0, keepdims=True) + EPSILON)
        answer = answer + alpha * direction
        if index + 1 < ITERS:
            resid = resid - alpha * image
            norm_next = jnp.sum(resid * resid, axis=0, keepdims=True)
            direction = resid + norm_next / (norm_now + EPSILON) * direction
            norm_now = norm_next
    out_ref[...] = answer.T

    for m in range(stages):
        own_to_sib(m).wait_send()
        for step in range(1, ny):
            y_copy(m, step).wait_send()
            x_copy(m, step, g).wait_send()
            f_copy(m, step, 0, far(step), g).wait_send()
            f_copy(m, step, 1, far(step), 1 - g).wait_send()


def local(items, item_factors, tile_lists, tile_weights, user_factors):
    rank = item_factors.shape[1]
    side = tile_weights.shape[-1]
    slots = tile_lists.shape[1]
    stages = side // ROWS
    far = items // 2 - 1
    shard = item_factors.reshape(-1, side, rank)
    tiles = shard.shape[0]
    dma = pltpu.SemaphoreType.DMA
    scratch = [pltpu.VMEM((items * tiles, ROWS, rank), F32) for _ in range(stages)]
    scratch += [
        pltpu.SMEM(tile_lists.shape, jnp.int32),
        pltpu.VMEM((slots, side, side), BF16),
        pltpu.VMEM((side, rank), F32),
        pltpu.VMEM((slots * side, side), F32),
        pltpu.VMEM((slots * side + rank, 2 * rank), BF16),
        pltpu.VMEM((2 * rank, slots * side), BF16),
        dma((3,)), dma((stages,)), dma((stages,)), dma((stages,)),
        dma((far, stages)), dma((far, stages)), dma((far, stages)), dma((far, stages)),
        dma((far, 2, stages)), dma((far, 2, stages)),
    ]
    hbm = pl.BlockSpec(memory_space=pl.ANY)
    return pl.pallas_call(
        functools.partial(kernel, items, stages),
        out_shape=jax.ShapeDtypeStruct((side, rank), F32),
        in_specs=[hbm, hbm, hbm, hbm],
        out_specs=pl.BlockSpec(memory_space=pltpu.VMEM),
        scratch_shapes=scratch,
        compiler_params=pltpu.CompilerParams(
            collective_id=0, has_side_effects=True, vmem_limit_bytes=63 * 1024 * 1024),
        name="half_sweep",
    )(tile_lists, shard, tile_weights.reshape(slots, side, side), user_factors)


def solution(mesh):
    in_specs = (
        P("item", None),
        P(("item", "user"), None),
        P(("item", "user"), None, None, None),
        P(("item", "user"), None),
    )
    out_specs = P(("item", "user"), None)
    body = functools.partial(local, mesh.shape["item"])
    return jax.shard_map(body, mesh=mesh, in_specs=in_specs, out_specs=out_specs, check_vma=False)
```

```python
import functools

import jax
import jax.numpy as jnp
from jax import lax
from jax.experimental import pallas as pl
from jax.experimental.pallas import tpu as pltpu
from jax.sharding import PartitionSpec as P

ITERS = 4
RIDGE_WEIGHT = 0.1
EPSILON = 1e-06
ROWS = 16
GROUP = 4
MESH = pl.DeviceIdType.MESH
F32 = jnp.float32
BF16 = jnp.bfloat16


def split(value):
    high = value.astype(BF16)
    low = (value - high.astype(F32)).astype(BF16)
    return high, low


def beside(value):
    return jnp.concatenate(split(value), axis=1)


def stacked(value):
    pair = beside(value)
    return jnp.concatenate([pair, pair], axis=0)


def dot(a, b):
    return jnp.dot(a, b, preferred_element_type=F32)


def fold_columns(value):
    half = value.shape[1] // 2
    return value[:, :half] + value[:, half:]


def fold_rows(value):
    half = value.shape[0] // 2
    return value[:half] + value[half:]


def kernel(items, stages, lists_hbm, shard_ref, w_ref, u_ref, out_ref, *scratch):
    bufs = scratch[:stages]
    (lists_ref, w_vm, u_vm, w_t, y_hl, y_t, in_sem, own_sem, sib_send, sib_recv, y_send, y_recv,
     g_send, g_recv, f_send, f_recv) = scratch[stages:]
    tiles = shard_ref.shape[0]
    slots = w_ref.shape[0]
    rank = shard_ref.shape[2]
    ny = items // 2
    piece = tiles // GROUP
    part_rows = slots * ROWS
    all_rows = stages * part_rows

    me = lax.axis_index("item")
    user = lax.axis_index("user")
    y, core = me // 2, lax.rem(me, 2)
    sibling = y * 2 + (1 - core)
    g = lax.rem(user, GROUP)
    g_low, g_high = lax.rem(g, 2), g // 2
    base = user - g
    parts = [g, g_high * 2 + (1 - g_low), (1 - g_high) * 2 + g_low, (1 - g_high) * 2 + (1 - g_low)]
    sib_id = (sibling, user)
    low_id = (me, base + parts[1])
    high_id = (me, base + parts[2])

    w_copy = pltpu.make_async_copy(w_ref, w_vm, in_sem.at[0])
    u_copy = pltpu.make_async_copy(u_ref, u_vm, in_sem.at[1])
    lists_copy = pltpu.make_async_copy(lists_hbm, lists_ref, in_sem.at[2])
    w_copy.start()
    u_copy.start()
    lists_copy.start()

    def y_id(step):
        return (lax.rem(y + step, ny) * 2 + core, user)

    barrier = pltpu.get_barrier_semaphore()
    pl.semaphore_signal(barrier, inc=1, device_id=sib_id, device_id_type=MESH)
    pl.semaphore_signal(barrier, inc=1, device_id=low_id, device_id_type=MESH)
    pl.semaphore_signal(barrier, inc=1, device_id=high_id, device_id_type=MESH)
    for step in range(1, ny):
        pl.semaphore_signal(barrier, inc=1, device_id=y_id(step), device_id_type=MESH)
    pl.semaphore_wait(barrier, 2 + ny)

    def remote(src, dst, send, recv, device):
        return pltpu.make_async_remote_copy(
            src_ref=src, dst_ref=dst, send_sem=send, recv_sem=recv,
            device_id=device, device_id_type=MESH)

    def region(m, shard, part=None, half=None):
        if part is None:
            return bufs[m].at[pl.ds(pl.multiple_of(shard * tiles, tiles), tiles)]
        first, count = shard * tiles + part * piece, piece
        if half is not None:
            count = piece // 2
            first = first + half * count
        return bufs[m].at[pl.ds(first, count)]

    def far(step):
        return lax.rem(y + ny - step, ny) * 2 + core

    def far_sib(step):
        return lax.rem(y + ny - step, ny) * 2 + (1 - core)

    def y_copy(m, step):
        mine = shard_ref.at[pl.ds(g * piece, piece), pl.ds(m * ROWS, ROWS)]
        return remote(mine, region(m, me, g),
                      y_send.at[step - 1, m], y_recv.at[step - 1, m], y_id(step))

    def y_arrival(m, step):
        place = region(m, far(step), g)
        return remote(place, place, y_send.at[step - 1, m], y_recv.at[step - 1, m], y_id(step))

    def g_copy(m, step, kind, part):
        place = region(m, far(step), part, None if kind < 2 else kind - 2)
        return remote(place, place, g_send.at[step - 1, kind, m], g_recv.at[step - 1, kind, m],
                      low_id if kind in (0, 3) else high_id)

    def f_copy(m, step, which, shard):
        place = region(m, shard, parts[which])
        return remote(place, place, f_send.at[step - 1, which, m], f_recv.at[step - 1, which, m], sib_id)

    def own_to_sib(m):
        return remote(shard_ref.at[:, pl.ds(m * ROWS, ROWS)], region(m, me),
                      sib_send.at[m], sib_recv.at[m], sib_id)

    def own_copy(m):
        return pltpu.make_async_copy(shard_ref.at[:, pl.ds(m * ROWS, ROWS)], region(m, me), own_sem.at[m])

    for m in range(stages):
        for step in range(1, ny):
            y_copy(m, step).start()
        own_to_sib(m).start()
        own_copy(m).start()

    w_copy.wait()
    for k in range(slots):
        turned = w_vm[k].astype(F32).T
        for m in range(stages):
            w_t[m * part_rows + k * ROWS:m * part_rows + (k + 1) * ROWS] = turned[m * ROWS:(m + 1) * ROWS]
    u_copy.wait()
    lists_copy.wait()
    answer = u_vm[...].T
    start_pair = stacked(answer)

    gram = jnp.zeros((rank, 2 * rank), F32)
    first = jnp.zeros((2 * rank, 2 * rank), F32)
    for turn in range(stages + 3):
        if turn < stages:
            m = turn
            for step in range(1, ny):
                y_arrival(m, step).wait_recv()
                g_copy(m, step, 0, parts[0]).start()
                g_copy(m, step, 1, parts[0]).start()
                f_copy(m, step, 0, far(step)).start()
        if 1 <= turn < stages + 1:
            m = turn - 1
            for step in range(1, ny):
                g_copy(m, step, 0, parts[1]).wait_recv()
                g_copy(m, step, 2, parts[1]).start()
                f_copy(m, step, 1, far(step)).start()
                g_copy(m, step, 1, parts[2]).wait_recv()
                g_copy(m, step, 3, parts[2]).start()
                f_copy(m, step, 2, far(step)).start()
        if 2 <= turn < stages + 2:
            m = turn - 2
            for step in range(1, ny):
                g_copy(m, step, 2, parts[3]).wait_recv()
                g_copy(m, step, 3, parts[3]).wait_recv()
                f_copy(m, step, 3, far(step)).start()
        if turn >= 3:
            m = turn - 3
            own_copy(m).wait()
            place = region(m, sibling)
            remote(place, place, sib_send.at[m], sib_recv.at[m], sib_id).wait_recv()
            for step in range(1, ny):
                for which in range(4):
                    f_copy(m, step, which, far_sib(step)).wait_recv()
            every, rest = split(bufs[m][...].reshape(-1, rank))
            gram += lax.dot_general(
                every, jnp.concatenate([every, rest], axis=1), (((0,), (0,)), ((), ())), preferred_element_type=F32)
            rows = jnp.concatenate([bufs[m][lists_ref[0, k]] for k in range(slots)], axis=0)
            rows_hl = beside(rows)
            columns_t = jnp.concatenate(split(rows.T), axis=0)
            span = slice(m * part_rows, (m + 1) * part_rows)
            y_hl[span] = rows_hl
            y_t[:, span] = columns_t
            scores = fold_columns(dot(rows_hl, start_pair))
            first += dot(columns_t, beside(1.0 + w_t[span] * (1.0 - scores)))

    gram_hl = beside(gram[:, :rank] + gram[:, rank:] + gram[:, rank:].T)
    y_hl[all_rows:] = gram_hl
    resid = fold_rows(fold_columns(first)) - fold_columns(dot(gram_hl, start_pair)) - RIDGE_WEIGHT * answer
    direction = resid
    norm_now = jnp.sum(resid * resid, axis=0, keepdims=True)
    for index in range(ITERS):
        scores = fold_columns(dot(y_hl[...], stacked(direction)))
        spread = dot(y_t[...], beside(scores[:all_rows] * w_t[...]))
        image = fold_rows(fold_columns(spread)) + scores[all_rows:] + RIDGE_WEIGHT * direction
        alpha = norm_now / (jnp.sum(direction * image, axis=0, keepdims=True) + EPSILON)
        answer = answer + alpha * direction
        if index + 1 < ITERS:
            resid = resid - alpha * image
            norm_next = jnp.sum(resid * resid, axis=0, keepdims=True)
            direction = resid + norm_next / (norm_now + EPSILON) * direction
            norm_now = norm_next
    out_ref[...] = answer.T

    for m in range(stages):
        own_to_sib(m).wait_send()
        for step in range(1, ny):
            y_copy(m, step).wait_send()
            for kind in range(4):
                g_copy(m, step, kind, parts[(0, 0, 1, 2)[kind]]).wait_send()
                f_copy(m, step, kind, far(step)).wait_send()


def local(items, item_factors, tile_lists, tile_weights, user_factors):
    rank = item_factors.shape[1]
    side = tile_weights.shape[-1]
    slots = tile_lists.shape[1]
    stages = side // ROWS
    far = items // 2 - 1
    shard = item_factors.reshape(-1, side, rank)
    tiles = shard.shape[0]
    dma = pltpu.SemaphoreType.DMA
    scratch = [pltpu.VMEM((items * tiles, ROWS, rank), F32) for _ in range(stages)]
    scratch += [
        pltpu.SMEM(tile_lists.shape, jnp.int32),
        pltpu.VMEM((slots, side, side), BF16),
        pltpu.VMEM((side, rank), F32),
        pltpu.VMEM((slots * side, side), F32),
        pltpu.VMEM((slots * side + rank, 2 * rank), BF16),
        pltpu.VMEM((2 * rank, slots * side), BF16),
        dma((3,)), dma((stages,)), dma((stages,)), dma((stages,)),
        dma((far, stages)), dma((far, stages)), dma((far, 4, stages)), dma((far, 4, stages)),
        dma((far, 4, stages)), dma((far, 4, stages)),
    ]
    hbm = pl.BlockSpec(memory_space=pl.ANY)
    return pl.pallas_call(
        functools.partial(kernel, items, stages),
        out_shape=jax.ShapeDtypeStruct((side, rank), F32),
        in_specs=[hbm, hbm, hbm, hbm],
        out_specs=pl.BlockSpec(memory_space=pltpu.VMEM),
        scratch_shapes=scratch,
        compiler_params=pltpu.CompilerParams(
            collective_id=0, has_side_effects=True, vmem_limit_bytes=63 * 1024 * 1024),
        name="half_sweep",
    )(tile_lists, shard, tile_weights.reshape(slots, side, side), user_factors)


def solution(mesh):
    in_specs = (
        P("item", None),
        P(("item", "user"), None),
        P(("item", "user"), None, None, None),
        P(("item", "user"), None),
    )
    out_specs = P(("item", "user"), None)
    body = functools.partial(local, mesh.shape["item"])
    return jax.shard_map(body, mesh=mesh, in_specs=in_specs, out_specs=out_specs, check_vma=False)
```

```python
import functools

import jax
import jax.numpy as jnp
from jax import lax
from jax.experimental import pallas as pl
from jax.experimental.pallas import tpu as pltpu
from jax.sharding import PartitionSpec as P

ITERS = 4
RIDGE_WEIGHT = 0.1
EPSILON = 1e-06
ROWS = 16
GROUP = 2
MESH = pl.DeviceIdType.MESH
F32 = jnp.float32
BF16 = jnp.bfloat16


def split(value):
    high = value.astype(BF16)
    low = (value - high.astype(F32)).astype(BF16)
    return high, low


def beside(value):
    return jnp.concatenate(split(value), axis=1)


def stacked(value):
    pair = beside(value)
    return jnp.concatenate([pair, pair], axis=0)


def dot(a, b):
    return jnp.dot(a, b, preferred_element_type=F32)


def fold_columns(value):
    half = value.shape[1] // 2
    return value[:, :half] + value[:, half:]


def fold_rows(value):
    half = value.shape[0] // 2
    return value[:half] + value[half:]


def kernel(items, stages, lists_hbm, shard_ref, w_ref, u_ref, out_ref, *scratch):
    bufs = scratch[:stages]
    (lists_ref, w_vm, u_vm, w_t, y_hl, y_t, grams, in_sem, own_sem, sib_send, sib_recv, y_send, y_recv,
     x_send, x_recv, f_send, f_recv, gs_sem, gy_send, gy_recv, gf_send, gf_recv) = scratch[stages:]
    tiles = shard_ref.shape[0]
    slots = w_ref.shape[0]
    rank = shard_ref.shape[2]
    ny = items // 2
    piece = ROWS // GROUP
    part_rows = slots * ROWS
    all_rows = stages * part_rows

    me = lax.axis_index("item")
    user = lax.axis_index("user")
    y, core = me // 2, lax.rem(me, 2)
    sibling = y * 2 + (1 - core)
    g = lax.rem(user, GROUP)
    peer = user - g + (1 - g)
    sib_id = (sibling, user)
    peer_id = (me, peer)

    w_copy = pltpu.make_async_copy(w_ref, w_vm, in_sem.at[0])
    u_copy = pltpu.make_async_copy(u_ref, u_vm, in_sem.at[1])
    lists_copy = pltpu.make_async_copy(lists_hbm, lists_ref, in_sem.at[2])
    w_copy.start()
    u_copy.start()
    lists_copy.start()

    def y_id(step):
        return (lax.rem(y + step, ny) * 2 + core, user)

    barrier = pltpu.get_barrier_semaphore()
    pl.semaphore_signal(barrier, inc=1, device_id=sib_id, device_id_type=MESH)
    pl.semaphore_signal(barrier, inc=1, device_id=peer_id, device_id_type=MESH)
    for step in range(1, ny):
        pl.semaphore_signal(barrier, inc=1, device_id=y_id(step), device_id_type=MESH)
    pl.semaphore_wait(barrier, 1 + ny)

    def remote(src, dst, send, recv, device):
        return pltpu.make_async_remote_copy(
            src_ref=src, dst_ref=dst, send_sem=send, recv_sem=recv,
            device_id=device, device_id_type=MESH)

    def region(m, shard, part=None):
        span = pl.ds(pl.multiple_of(shard * tiles, tiles), tiles)
        if part is None:
            return bufs[m].at[span]
        return bufs[m].at[span, pl.ds(pl.multiple_of(part * piece, piece), piece)]

    def far(step):
        return lax.rem(y + ny - step, ny) * 2 + core

    def far_sib(step):
        return lax.rem(y + ny - step, ny) * 2 + (1 - core)

    def y_copy(m, step):
        rows = pl.ds(pl.multiple_of(m * ROWS + g * piece, piece), piece)
        return remote(shard_ref.at[:, rows], region(m, me, g),
                      y_send.at[step - 1, m], y_recv.at[step - 1, m], y_id(step))

    def y_arrival(m, step):
        place = region(m, far(step), g)
        return remote(place, place, y_send.at[step - 1, m], y_recv.at[step - 1, m], y_id(step))

    def x_copy(m, step, part):
        place = region(m, far(step), part)
        return remote(place, place, x_send.at[step - 1, m], x_recv.at[step - 1, m], peer_id)

    def f_copy(m, step, which, shard, part):
        place = region(m, shard, part)
        return remote(place, place, f_send.at[step - 1, which, m], f_recv.at[step - 1, which, m], sib_id)

    def own_to_sib(m):
        return remote(shard_ref.at[:, pl.ds(m * ROWS, ROWS)], region(m, me),
                      sib_send.at[m], sib_recv.at[m], sib_id)

    def own_copy(m):
        return pltpu.make_async_copy(shard_ref.at[:, pl.ds(m * ROWS, ROWS)], region(m, me), own_sem.at[m])

    def gram_copy(shard, send, recv, device):
        return remote(grams.at[shard], grams.at[shard], send, recv, device)

    for m in range(stages):
        for step in range(1, ny):
            y_copy(m, step).start()
        own_to_sib(m).start()
        own_copy(m).start()

    part = jnp.zeros((rank, 2 * rank), F32)
    for m in range(stages):
        own_copy(m).wait()
        mine = bufs[m][pl.ds(pl.multiple_of(me * tiles, tiles), tiles)]
        high, low = split(mine.reshape(-1, rank))
        part += lax.dot_general(
            high, jnp.concatenate([high, low], axis=1), (((0,), (0,)), ((), ())), preferred_element_type=F32)
    grams[me] = part[:, :rank] + part[:, rank:] + part[:, rank:].T
    gram_copy(me, gs_sem.at[0], gs_sem.at[1], sib_id).start()
    for step in range(1, ny):
        gram_copy(me, gy_send.at[step - 1], gy_recv.at[step - 1], y_id(step)).start()

    w_copy.wait()
    for k in range(slots):
        turned = w_vm[k].astype(F32).T
        for m in range(stages):
            w_t[m * part_rows + k * ROWS:m * part_rows + (k + 1) * ROWS] = turned[m * ROWS:(m + 1) * ROWS]
    u_copy.wait()
    lists_copy.wait()
    answer = u_vm[...].T
    start_pair = stacked(answer)

    first = jnp.zeros((2 * rank, 2 * rank), F32)
    for turn in range(stages + 2):
        if turn < stages:
            for step in range(1, ny):
                y_arrival(turn, step).wait_recv()
                x_copy(turn, step, g).start()
                f_copy(turn, step, 0, far(step), g).start()
        if 1 <= turn <= stages:
            for step in range(1, ny):
                x_copy(turn - 1, step, 1 - g).wait_recv()
                f_copy(turn - 1, step, 1, far(step), 1 - g).start()
        if turn >= 2:
            m = turn - 2
            place = region(m, sibling)
            remote(place, place, sib_send.at[m], sib_recv.at[m], sib_id).wait_recv()
            for step in range(1, ny):
                f_copy(m, step, 0, far_sib(step), g).wait_recv()
                f_copy(m, step, 1, far_sib(step), 1 - g).wait_recv()
            rows = jnp.concatenate([bufs[m][lists_ref[0, k]] for k in range(slots)], axis=0)
            rows_hl = beside(rows)
            columns_t = jnp.concatenate(split(rows.T), axis=0)
            span = slice(m * part_rows, (m + 1) * part_rows)
            y_hl[span] = rows_hl
            y_t[:, span] = columns_t
            scores = fold_columns(dot(rows_hl, start_pair))
            first += dot(columns_t, beside(1.0 + w_t[span] * (1.0 - scores)))

    for step in range(1, ny):
        gram_copy(far(step), gy_send.at[step - 1], gy_recv.at[step - 1], y_id(step)).wait_recv()
        gram_copy(far(step), gf_send.at[step - 1], gf_recv.at[step - 1], sib_id).start()
    gram_copy(sibling, gs_sem.at[0], gs_sem.at[1], sib_id).wait_recv()
    for step in range(1, ny):
        gram_copy(far_sib(step), gf_send.at[step - 1], gf_recv.at[step - 1], sib_id).wait_recv()
    gram_hl = beside(jnp.sum(grams[...], axis=0))
    y_hl[all_rows:] = gram_hl
    resid = fold_rows(fold_columns(first)) - fold_columns(dot(gram_hl, start_pair)) - RIDGE_WEIGHT * answer
    direction = resid
    norm_now = jnp.sum(resid * resid, axis=0, keepdims=True)
    for index in range(ITERS):
        scores = fold_columns(dot(y_hl[...], stacked(direction)))
        weighted = scores[:all_rows] * w_t[...]
        image = scores[all_rows:] + RIDGE_WEIGHT * direction
        curve = jnp.zeros_like(norm_now)
        if index + 1 < ITERS:
            image += fold_rows(fold_columns(dot(y_t[...], beside(weighted))))
        else:
            curve = jnp.sum(weighted * scores[:all_rows], axis=0, keepdims=True)
        alpha = norm_now / (curve + jnp.sum(direction * image, axis=0, keepdims=True) + EPSILON)
        answer = answer + alpha * direction
        if index + 1 < ITERS:
            resid = resid - alpha * image
            norm_next = jnp.sum(resid * resid, axis=0, keepdims=True)
            direction = resid + norm_next / (norm_now + EPSILON) * direction
            norm_now = norm_next
    out_ref[...] = answer.T

    gram_copy(me, gs_sem.at[0], gs_sem.at[1], sib_id).wait_send()
    for step in range(1, ny):
        gram_copy(me, gy_send.at[step - 1], gy_recv.at[step - 1], y_id(step)).wait_send()
        gram_copy(far(step), gf_send.at[step - 1], gf_recv.at[step - 1], sib_id).wait_send()
    for m in range(stages):
        own_to_sib(m).wait_send()
        for step in range(1, ny):
            y_copy(m, step).wait_send()
            x_copy(m, step, g).wait_send()
            f_copy(m, step, 0, far(step), g).wait_send()
            f_copy(m, step, 1, far(step), 1 - g).wait_send()


def local(items, item_factors, tile_lists, tile_weights, user_factors):
    rank = item_factors.shape[1]
    side = tile_weights.shape[-1]
    slots = tile_lists.shape[1]
    stages = side // ROWS
    far = items // 2 - 1
    shard = item_factors.reshape(-1, side, rank)
    tiles = shard.shape[0]
    dma = pltpu.SemaphoreType.DMA
    scratch = [pltpu.VMEM((items * tiles, ROWS, rank), F32) for _ in range(stages)]
    scratch += [
        pltpu.SMEM(tile_lists.shape, jnp.int32),
        pltpu.VMEM((slots, side, side), BF16),
        pltpu.VMEM((side, rank), F32),
        pltpu.VMEM((slots * side, side), F32),
        pltpu.VMEM((slots * side + rank, 2 * rank), BF16),
        pltpu.VMEM((2 * rank, slots * side), BF16),
        pltpu.VMEM((items, rank, rank), F32),
        dma((3,)), dma((stages,)), dma((stages,)), dma((stages,)),
        dma((far, stages)), dma((far, stages)), dma((far, stages)), dma((far, stages)),
        dma((far, 2, stages)), dma((far, 2, stages)),
        dma((2,)), dma((far,)), dma((far,)), dma((far,)), dma((far,)),
    ]
    hbm = pl.BlockSpec(memory_space=pl.ANY)
    return pl.pallas_call(
        functools.partial(kernel, items, stages),
        out_shape=jax.ShapeDtypeStruct((side, rank), F32),
        in_specs=[hbm, hbm, hbm, hbm],
        out_specs=pl.BlockSpec(memory_space=pltpu.VMEM),
        scratch_shapes=scratch,
        compiler_params=pltpu.CompilerParams(
            collective_id=0, has_side_effects=True, vmem_limit_bytes=63 * 1024 * 1024),
        name="half_sweep",
    )(tile_lists, shard, tile_weights.reshape(slots, side, side), user_factors)


def solution(mesh):
    in_specs = (
        P("item", None),
        P(("item", "user"), None),
        P(("item", "user"), None, None, None),
        P(("item", "user"), None),
    )
    out_specs = P(("item", "user"), None)
    body = functools.partial(local, mesh.shape["item"])
    return jax.shard_map(body, mesh=mesh, in_specs=in_specs, out_specs=out_specs, check_vma=False)
```

```python
import functools

import jax
import jax.numpy as jnp
from jax import lax
from jax.experimental import pallas as pl
from jax.experimental.pallas import tpu as pltpu
from jax.sharding import PartitionSpec as P

ITERS = 4
RIDGE_WEIGHT = 0.1
EPSILON = 1e-06
ROWS = 16
GROUP = 2
MESH = pl.DeviceIdType.MESH
F32 = jnp.float32
BF16 = jnp.bfloat16


def split(value):
    high = value.astype(BF16)
    low = (value - high.astype(F32)).astype(BF16)
    return high, low


def beside(value):
    return jnp.concatenate(split(value), axis=1)


def stacked(value):
    pair = beside(value)
    return jnp.concatenate([pair, pair], axis=0)


def dot(a, b):
    return jnp.dot(a, b, preferred_element_type=F32)


def fold_columns(value):
    half = value.shape[1] // 2
    return value[:, :half] + value[:, half:]


def fold_rows(value):
    half = value.shape[0] // 2
    return value[:half] + value[half:]


def kernel(items, stages, lists_hbm, shard_ref, w_ref, u_ref, out_ref, *scratch):
    bufs, packs, lands = scratch[:stages], scratch[stages:2 * stages], scratch[2 * stages:3 * stages]
    (lists_ref, sib_lists, w_vm, u_vm, w_t, y_hl, y_t, grams, in_sem, own_sem, sib_send, sib_recv, y_send, y_recv,
     x_send, x_recv, gs_sem, gy_send, gy_recv, gf_send, gf_recv, l_sem) = scratch[3 * stages:]
    tiles = shard_ref.shape[0]
    slots = w_ref.shape[0]
    rank = shard_ref.shape[2]
    ny = items // 2
    piece = ROWS // GROUP
    part_rows = slots * ROWS
    all_rows = stages * part_rows

    me = lax.axis_index("item")
    user = lax.axis_index("user")
    y, core = me // 2, lax.rem(me, 2)
    sibling = y * 2 + (1 - core)
    g = lax.rem(user, GROUP)
    peer = user - g + (1 - g)
    sib_id = (sibling, user)
    peer_id = (me, peer)

    w_copy = pltpu.make_async_copy(w_ref, w_vm, in_sem.at[0])
    u_copy = pltpu.make_async_copy(u_ref, u_vm, in_sem.at[1])
    lists_copy = pltpu.make_async_copy(lists_hbm, lists_ref, in_sem.at[2])
    w_copy.start()
    u_copy.start()
    lists_copy.start()

    def y_id(step):
        return (lax.rem(y + step, ny) * 2 + core, user)

    barrier = pltpu.get_barrier_semaphore()
    pl.semaphore_signal(barrier, inc=1, device_id=sib_id, device_id_type=MESH)
    pl.semaphore_signal(barrier, inc=1, device_id=peer_id, device_id_type=MESH)
    for step in range(1, ny):
        pl.semaphore_signal(barrier, inc=1, device_id=y_id(step), device_id_type=MESH)
    pl.semaphore_wait(barrier, 1 + ny)

    def remote(src, dst, send, recv, device):
        return pltpu.make_async_remote_copy(
            src_ref=src, dst_ref=dst, send_sem=send, recv_sem=recv,
            device_id=device, device_id_type=MESH)

    def region(m, shard, part=None):
        span = pl.ds(pl.multiple_of(shard // 2 * tiles, tiles), tiles)
        if part is None:
            return bufs[m].at[span]
        return bufs[m].at[span, pl.ds(pl.multiple_of(part * piece, piece), piece)]

    def far(step):
        return lax.rem(y + ny - step, ny) * 2 + core

    def far_sib(step):
        return lax.rem(y + ny - step, ny) * 2 + (1 - core)

    def y_copy(m, step):
        rows = pl.ds(pl.multiple_of(m * ROWS + g * piece, piece), piece)
        return remote(shard_ref.at[:, rows], region(m, me, g),
                      y_send.at[step - 1, m], y_recv.at[step - 1, m], y_id(step))

    def y_arrival(m, step):
        place = region(m, far(step), g)
        return remote(place, place, y_send.at[step - 1, m], y_recv.at[step - 1, m], y_id(step))

    def x_copy(m, step, part):
        place = region(m, far(step), part)
        return remote(place, place, x_send.at[step - 1, m], x_recv.at[step - 1, m], peer_id)

    def f_copy(m):
        return remote(packs[m], lands[m], sib_send.at[m], sib_recv.at[m], sib_id)

    def place(tile):
        return tile // (2 * tiles) * tiles + tile % tiles

    def own_copy(m):
        return pltpu.make_async_copy(shard_ref.at[:, pl.ds(m * ROWS, ROWS)], region(m, me), own_sem.at[m])

    list_copy = remote(lists_hbm, sib_lists, l_sem.at[0], l_sem.at[1], sib_id)
    list_copy.start()

    def gram_copy(shard, send, recv, device):
        return remote(grams.at[shard], grams.at[shard], send, recv, device)

    for m in range(stages):
        for step in range(1, ny):
            y_copy(m, step).start()
        own_copy(m).start()

    part = jnp.zeros((rank, 2 * rank), F32)
    for m in range(stages):
        own_copy(m).wait()
        mine = bufs[m][pl.ds(pl.multiple_of(y * tiles, tiles), tiles)]
        high, low = split(mine.reshape(-1, rank))
        part += lax.dot_general(
            high, jnp.concatenate([high, low], axis=1), (((0,), (0,)), ((), ())), preferred_element_type=F32)
    grams[me] = part[:, :rank] + part[:, rank:] + part[:, rank:].T
    gram_copy(me, gs_sem.at[0], gs_sem.at[1], sib_id).start()
    for step in range(1, ny):
        gram_copy(me, gy_send.at[step - 1], gy_recv.at[step - 1], y_id(step)).start()

    w_copy.wait()
    for k in range(slots):
        turned = w_vm[k].astype(F32).T
        for m in range(stages):
            w_t[m * part_rows + k * ROWS:m * part_rows + (k + 1) * ROWS] = turned[m * ROWS:(m + 1) * ROWS]
    u_copy.wait()
    lists_copy.wait()
    list_copy.wait()
    here = [place(lists_ref[0, k]) for k in range(slots)]
    there = [place(sib_lists[0, k]) for k in range(slots)]
    local = [lists_ref[0, k] // tiles % 2 == core for k in range(slots)]
    answer = u_vm[...].T
    start_pair = stacked(answer)

    first = jnp.zeros((2 * rank, 2 * rank), F32)
    for turn in range(stages + 2):
        if turn < stages:
            for step in range(1, ny):
                y_arrival(turn, step).wait_recv()
                x_copy(turn, step, g).start()
        if 1 <= turn <= stages:
            for step in range(1, ny):
                x_copy(turn - 1, step, 1 - g).wait_recv()
            for k in range(slots):
                packs[turn - 1][k] = bufs[turn - 1][there[k]]
            f_copy(turn - 1).start()
        if turn >= 2:
            m = turn - 2
            f_copy(m).wait_recv()
            rows = jnp.concatenate(
                [jnp.where(local[k], bufs[m][here[k]], lands[m][k]) for k in range(slots)], axis=0)
            rows_hl = beside(rows)
            columns_t = jnp.concatenate(split(rows.T), axis=0)
            span = slice(m * part_rows, (m + 1) * part_rows)
            y_hl[span] = rows_hl
            y_t[:, span] = columns_t
            scores = fold_columns(dot(rows_hl, start_pair))
            first += dot(columns_t, beside(1.0 + w_t[span] * (1.0 - scores)))

    for step in range(1, ny):
        gram_copy(far(step), gy_send.at[step - 1], gy_recv.at[step - 1], y_id(step)).wait_recv()
        gram_copy(far(step), gf_send.at[step - 1], gf_recv.at[step - 1], sib_id).start()
    gram_copy(sibling, gs_sem.at[0], gs_sem.at[1], sib_id).wait_recv()
    for step in range(1, ny):
        gram_copy(far_sib(step), gf_send.at[step - 1], gf_recv.at[step - 1], sib_id).wait_recv()
    gram_hl = beside(jnp.sum(grams[...], axis=0))
    y_hl[all_rows:] = gram_hl
    resid = fold_rows(fold_columns(first)) - fold_columns(dot(gram_hl, start_pair)) - RIDGE_WEIGHT * answer
    direction = resid
    norm_now = jnp.sum(resid * resid, axis=0, keepdims=True)
    for index in range(ITERS):
        scores = fold_columns(dot(y_hl[...], stacked(direction)))
        weighted = scores[:all_rows] * w_t[...]
        image = scores[all_rows:] + RIDGE_WEIGHT * direction
        curve = jnp.zeros_like(norm_now)
        if index + 1 < ITERS:
            image += fold_rows(fold_columns(dot(y_t[...], beside(weighted))))
        else:
            curve = jnp.sum(weighted * scores[:all_rows], axis=0, keepdims=True)
        alpha = norm_now / (curve + jnp.sum(direction * image, axis=0, keepdims=True) + EPSILON)
        answer = answer + alpha * direction
        if index + 1 < ITERS:
            resid = resid - alpha * image
            norm_next = jnp.sum(resid * resid, axis=0, keepdims=True)
            direction = resid + norm_next / (norm_now + EPSILON) * direction
            norm_now = norm_next
    out_ref[...] = answer.T

    gram_copy(me, gs_sem.at[0], gs_sem.at[1], sib_id).wait_send()
    for step in range(1, ny):
        gram_copy(me, gy_send.at[step - 1], gy_recv.at[step - 1], y_id(step)).wait_send()
        gram_copy(far(step), gf_send.at[step - 1], gf_recv.at[step - 1], sib_id).wait_send()
    for m in range(stages):
        f_copy(m).wait_send()
        for step in range(1, ny):
            y_copy(m, step).wait_send()
            x_copy(m, step, g).wait_send()


def local(items, item_factors, tile_lists, tile_weights, user_factors):
    rank = item_factors.shape[1]
    side = tile_weights.shape[-1]
    slots = tile_lists.shape[1]
    stages = side // ROWS
    far = items // 2 - 1
    shard = item_factors.reshape(-1, side, rank)
    tiles = shard.shape[0]
    dma = pltpu.SemaphoreType.DMA
    scratch = [pltpu.VMEM((items // 2 * tiles, ROWS, rank), F32) for _ in range(stages)]
    scratch += [pltpu.VMEM((slots, ROWS, rank), F32) for _ in range(2 * stages)]
    scratch += [
        pltpu.SMEM(tile_lists.shape, jnp.int32),
        pltpu.SMEM(tile_lists.shape, jnp.int32),
        pltpu.VMEM((slots, side, side), BF16),
        pltpu.VMEM((side, rank), F32),
        pltpu.VMEM((slots * side, side), F32),
        pltpu.VMEM((slots * side + rank, 2 * rank), BF16),
        pltpu.VMEM((2 * rank, slots * side), BF16),
        pltpu.VMEM((items, rank, rank), F32),
        dma((3,)), dma((stages,)), dma((stages,)), dma((stages,)),
        dma((far, stages)), dma((far, stages)), dma((far, stages)), dma((far, stages)),
        dma((2,)), dma((far,)), dma((far,)), dma((far,)), dma((far,)), dma((2,)),
    ]
    hbm = pl.BlockSpec(memory_space=pl.ANY)
    return pl.pallas_call(
        functools.partial(kernel, items, stages),
        out_shape=jax.ShapeDtypeStruct((side, rank), F32),
        in_specs=[hbm, hbm, hbm, hbm],
        out_specs=pl.BlockSpec(memory_space=pltpu.VMEM),
        scratch_shapes=scratch,
        compiler_params=pltpu.CompilerParams(
            collective_id=0, has_side_effects=True, vmem_limit_bytes=63 * 1024 * 1024),
        name="half_sweep",
    )(tile_lists, shard, tile_weights.reshape(slots, side, side), user_factors)


def solution(mesh):
    in_specs = (
        P("item", None),
        P(("item", "user"), None),
        P(("item", "user"), None, None, None),
        P(("item", "user"), None),
    )
    out_specs = P(("item", "user"), None)
    body = functools.partial(local, mesh.shape["item"])
    return jax.shard_map(body, mesh=mesh, in_specs=in_specs, out_specs=out_specs, check_vma=False)
```

```python
import functools

import jax
import jax.numpy as jnp
from jax import lax
from jax.experimental import pallas as pl
from jax.experimental.pallas import tpu as pltpu
from jax.sharding import PartitionSpec as P

ITERS = 4
RIDGE_WEIGHT = 0.1
EPSILON = 1e-06
ROWS = 16
GROUP = 2
MESH = pl.DeviceIdType.MESH
F32 = jnp.float32
BF16 = jnp.bfloat16


def split(value):
    high = value.astype(BF16)
    low = (value - high.astype(F32)).astype(BF16)
    return high, low


def beside(value):
    return jnp.concatenate(split(value), axis=1)


def stacked(value):
    pair = beside(value)
    return jnp.concatenate([pair, pair], axis=0)


def dot(a, b):
    return jnp.dot(a, b, preferred_element_type=F32)


def fold_columns(value):
    half = value.shape[1] // 2
    return value[:, :half] + value[:, half:]


def fold_rows(value):
    half = value.shape[0] // 2
    return value[:half] + value[half:]


def kernel(items, stages, lists_hbm, shard_ref, w_ref, u_ref, out_ref, *scratch):
    bufs = scratch[:stages]
    (lists_ref, w_vm, u_vm, w_t, y_hl, y_t, in_sem, own_sem, sib_send, sib_recv, y_send, y_recv,
     x_send, x_recv, f_send, f_recv) = scratch[stages:]
    tiles = shard_ref.shape[0]
    slots = w_ref.shape[0]
    rank = shard_ref.shape[2]
    ny = items // 2
    piece = ROWS // GROUP
    part_rows = slots * ROWS
    all_rows = stages * part_rows

    me = lax.axis_index("item")
    user = lax.axis_index("user")
    y, core = me // 2, lax.rem(me, 2)
    sibling = y * 2 + (1 - core)
    g = lax.rem(user, GROUP)
    peer = user - g + (1 - g)
    sib_id = (sibling, user)
    peer_id = (me, peer)

    w_copy = pltpu.make_async_copy(w_ref, w_vm, in_sem.at[0])
    u_copy = pltpu.make_async_copy(u_ref, u_vm, in_sem.at[1])
    lists_copy = pltpu.make_async_copy(lists_hbm, lists_ref, in_sem.at[2])
    w_copy.start()
    u_copy.start()
    lists_copy.start()

    def y_id(step):
        return (lax.rem(y + step, ny) * 2 + core, user)

    barrier = pltpu.get_barrier_semaphore()
    pl.semaphore_signal(barrier, inc=1, device_id=sib_id, device_id_type=MESH)
    pl.semaphore_signal(barrier, inc=1, device_id=peer_id, device_id_type=MESH)
    for step in range(1, ny):
        pl.semaphore_signal(barrier, inc=1, device_id=y_id(step), device_id_type=MESH)
    pl.semaphore_wait(barrier, 1 + ny)

    def remote(src, dst, send, recv, device):
        return pltpu.make_async_remote_copy(
            src_ref=src, dst_ref=dst, send_sem=send, recv_sem=recv,
            device_id=device, device_id_type=MESH)

    def region(m, shard, part=None):
        span = pl.ds(pl.multiple_of(shard * tiles, tiles), tiles)
        if part is None:
            return bufs[m].at[span]
        return bufs[m].at[span, pl.ds(pl.multiple_of(part * piece, piece), piece)]

    def far(step):
        return lax.rem(y + ny - step, ny) * 2 + core

    def far_sib(step):
        return lax.rem(y + ny - step, ny) * 2 + (1 - core)

    def y_copy(m, step):
        rows = pl.ds(pl.multiple_of(m * ROWS + g * piece, piece), piece)
        return remote(shard_ref.at[:, rows], region(m, me, g),
                      y_send.at[step - 1, m], y_recv.at[step - 1, m], y_id(step))

    def y_arrival(m, step):
        place = region(m, far(step), g)
        return remote(place, place, y_send.at[step - 1, m], y_recv.at[step - 1, m], y_id(step))

    def x_copy(m, step, part):
        place = region(m, far(step), part)
        return remote(place, place, x_send.at[step - 1, m], x_recv.at[step - 1, m], peer_id)

    def f_copy(m, step, which, shard, part):
        place = region(m, shard, part)
        return remote(place, place, f_send.at[step - 1, which, m], f_recv.at[step - 1, which, m], sib_id)

    def own_to_sib(m):
        return remote(shard_ref.at[:, pl.ds(m * ROWS, ROWS)], region(m, me),
                      sib_send.at[m], sib_recv.at[m], sib_id)

    def own_copy(m):
        return pltpu.make_async_copy(shard_ref.at[:, pl.ds(m * ROWS, ROWS)], region(m, me), own_sem.at[m])

    for m in range(stages):
        for step in range(1, ny):
            y_copy(m, step).start()
        own_to_sib(m).start()
        own_copy(m).start()

    w_copy.wait()
    for k in range(slots):
        turned = w_vm[k].astype(F32).T
        for m in range(stages):
            w_t[m * part_rows + k * ROWS:m * part_rows + (k + 1) * ROWS] = turned[m * ROWS:(m + 1) * ROWS]
    u_copy.wait()
    lists_copy.wait()
    answer = u_vm[...].T
    start_pair = stacked(answer)

    gram = jnp.zeros((rank, 2 * rank), F32)
    first = jnp.zeros((2 * rank, 2 * rank), F32)
    for turn in range(stages + 2):
        if turn < stages:
            for step in range(1, ny):
                y_arrival(turn, step).wait_recv()
                x_copy(turn, step, g).start()
                f_copy(turn, step, 0, far(step), g).start()
        if 1 <= turn <= stages:
            for step in range(1, ny):
                x_copy(turn - 1, step, 1 - g).wait_recv()
                f_copy(turn - 1, step, 1, far(step), 1 - g).start()
        if turn >= 2:
            m = turn - 2
            own_copy(m).wait()
            place = region(m, sibling)
            remote(place, place, sib_send.at[m], sib_recv.at[m], sib_id).wait_recv()
            for step in range(1, ny):
                f_copy(m, step, 0, far_sib(step), g).wait_recv()
                f_copy(m, step, 1, far_sib(step), 1 - g).wait_recv()
            every, rest = split(bufs[m][...].reshape(-1, rank))
            gram += lax.dot_general(
                every, jnp.concatenate([every, rest], axis=1), (((0,), (0,)), ((), ())), preferred_element_type=F32)
            rows = jnp.concatenate([bufs[m][lists_ref[0, k]] for k in range(slots)], axis=0)
            rows_hl = beside(rows)
            columns_t = jnp.concatenate(split(rows.T), axis=0)
            span = slice(m * part_rows, (m + 1) * part_rows)
            y_hl[span] = rows_hl
            y_t[:, span] = columns_t
            scores = fold_columns(dot(rows_hl, start_pair))
            first += dot(columns_t, beside(1.0 + w_t[span] * (1.0 - scores)))

    gram_hl = beside(gram[:, :rank] + gram[:, rank:] + gram[:, rank:].T)
    y_hl[all_rows:] = gram_hl
    resid = fold_rows(fold_columns(first)) - fold_columns(dot(gram_hl, start_pair)) - RIDGE_WEIGHT * answer
    direction = resid
    norm_now = jnp.sum(resid * resid, axis=0, keepdims=True)
    for index in range(ITERS):
        scores = fold_columns(dot(y_hl[...], stacked(direction)))
        weighted = scores[:all_rows] * w_t[...]
        image = scores[all_rows:] + RIDGE_WEIGHT * direction
        curve = jnp.zeros_like(norm_now)
        if index + 1 < ITERS:
            image += fold_rows(fold_columns(dot(y_t[...], beside(weighted))))
        else:
            curve = jnp.sum(weighted * scores[:all_rows], axis=0, keepdims=True)
        alpha = norm_now / (curve + jnp.sum(direction * image, axis=0, keepdims=True) + EPSILON)
        answer = answer + alpha * direction
        if index + 1 < ITERS:
            resid = resid - alpha * image
            norm_next = jnp.sum(resid * resid, axis=0, keepdims=True)
            direction = resid + norm_next / (norm_now + EPSILON) * direction
            norm_now = norm_next
    out_ref[...] = answer.T

    for m in range(stages):
        own_to_sib(m).wait_send()
        for step in range(1, ny):
            y_copy(m, step).wait_send()
            x_copy(m, step, g).wait_send()
            f_copy(m, step, 0, far(step), g).wait_send()
            f_copy(m, step, 1, far(step), 1 - g).wait_send()


def local(items, item_factors, tile_lists, tile_weights, user_factors):
    rank = item_factors.shape[1]
    side = tile_weights.shape[-1]
    slots = tile_lists.shape[1]
    stages = side // ROWS
    far = items // 2 - 1
    shard = item_factors.reshape(-1, side, rank)
    tiles = shard.shape[0]
    dma = pltpu.SemaphoreType.DMA
    scratch = [pltpu.VMEM((items * tiles, ROWS, rank), F32) for _ in range(stages)]
    scratch += [
        pltpu.SMEM(tile_lists.shape, jnp.int32),
        pltpu.VMEM((slots, side, side), BF16),
        pltpu.VMEM((side, rank), F32),
        pltpu.VMEM((slots * side, side), F32),
        pltpu.VMEM((slots * side + rank, 2 * rank), BF16),
        pltpu.VMEM((2 * rank, slots * side), BF16),
        dma((3,)), dma((stages,)), dma((stages,)), dma((stages,)),
        dma((far, stages)), dma((far, stages)), dma((far, stages)), dma((far, stages)),
        dma((far, 2, stages)), dma((far, 2, stages)),
    ]
    hbm = pl.BlockSpec(memory_space=pl.ANY)
    return pl.pallas_call(
        functools.partial(kernel, items, stages),
        out_shape=jax.ShapeDtypeStruct((side, rank), F32),
        in_specs=[hbm, hbm, hbm, hbm],
        out_specs=pl.BlockSpec(memory_space=pltpu.VMEM),
        scratch_shapes=scratch,
        compiler_params=pltpu.CompilerParams(
            collective_id=0, has_side_effects=True, vmem_limit_bytes=63 * 1024 * 1024),
        name="half_sweep",
    )(tile_lists, shard, tile_weights.reshape(slots, side, side), user_factors)


def solution(mesh):
    in_specs = (
        P("item", None),
        P(("item", "user"), None),
        P(("item", "user"), None, None, None),
        P(("item", "user"), None),
    )
    out_specs = P(("item", "user"), None)
    body = functools.partial(local, mesh.shape["item"])
    return jax.shard_map(body, mesh=mesh, in_specs=in_specs, out_specs=out_specs, check_vma=False)
```
